32 devices in a mesh: temp: 4 (over y, core), dom: 8 (over z, x).
Axes of the slice: x: 2, y: 2, z: 4, core: 2. Of those that a mesh axis runs over, the one named last changes fastest.
Arguments:
- particles: bfloat16 [4, 4096, 3072], P('temp', 'dom'), may hold values from -6 to 6
- log_weights: float32 [4, 4096], P('temp', 'dom'), may hold values from -200 to 200
- offspring: int32 [4, 64], P('temp', 'dom'), may hold values from 0 to 2, as said below
- even_pairs: int32 [4, 64], P('temp', 'dom'), may hold values from 0 to 1, as said below
- odd_pairs: int32 [4, 64], P('temp', 'dom'), may hold values from 0 to 1, as said below
- inverse_temp: float32 [4], P('temp'), may hold values from 0.5 to 4
- flow_in: bfloat16 [1536, 512], replicated, may hold values from -0.15625 to 0.15625
- flow_mid: bfloat16 [512, 512], replicated, may hold values from -0.25 to 0.25
- flow_out: bfloat16 [512, 3072], replicated, may hold values from -0.25 to 0.25
- energy_in: bfloat16 [3072, 512], replicated, may hold values from -0.109375 to 0.109375
- energy_mid: bfloat16 [512, 512], replicated, may hold values from -0.25 to 0.25
- energy_out: float32 [512], replicated, may hold values from -0.25 to 0.25
Outputs:
- new_particles: bfloat16 [4, 4096, 3072], P('temp', 'dom')
- new_log_weights: float32 [4, 4096], P('temp', 'dom')
- log_ess: float32 [4], P('temp')
The draws below stay inside these ranges and needn't reach their ends.
Inputs may be any that keep to these rules, and one draw needn't show every extreme that they name: `offspring`: counts are 0, 1 or 2 and each group's counts sum to 64. Of the 8 blocks of one device at most 1 have count 2 and at most 1 have count 0; in every group some device has exactly 1 with count 2 and some device exactly 1 with count 0. `even_pairs`: groups 2i and 2i + 1 carry equal rows. At most 2 of the 8 blocks of one device are 1, and in every pair some device has exactly 2. `odd_pairs`: groups 2i + 1 and 2i + 2 carry equal rows; groups 0 and 3 are all 0. At most 2 of the 8 blocks of one device are 1, and in every pair some device has exactly 2.
All inputs are finite; a program needn't handle non-finite values.
Results may differ from the reference program's by a relative error of at most 0.0024.
Values may be sent and summed in bfloat16 or wider, within the bound.
A program may use at most 128 MiB of HBM per device.

```python
import math
import jax
import jax.numpy as jnp
from jax import lax

DIM = 3072
HID = 512
SURPLUS = 1
SWAPS = 2
BLK_DEV = 8
GROUPS = 4
NBLK = 64
PARTICLES = 4096


def draw_log_weights(key, part):
    key_one = jax.random.fold_in(key, 0)
    position = jnp.arange(PARTICLES, dtype=jnp.float32) / (PARTICLES - 1)
    noise = jax.random.normal(key_one, (GROUPS, PARTICLES), jnp.float32)
    return (noise + jnp.log(1.0 + 2.0 * position)[None, :]).astype(jnp.float32)


def draw_offspring(key, part):
    devices = NBLK // BLK_DEV
    half_devices = devices // 2
    key_one, key_two, key_three, key_four, key_five, key_six = jax.random.split(key, 6)
    device_ids = jnp.arange(devices)
    surplus_rows = jax.random.randint(key_one, (GROUPS, devices), 0, SURPLUS + 1)
    forced = jax.random.randint(key_two, (GROUPS,), 0, half_devices)
    surplus_rows = jnp.where(device_ids[None, :] == forced[:, None], SURPLUS, surplus_rows)
    random_permute = jax.vmap(lambda subkey: jax.random.permutation(subkey, devices))(jax.random.split(key_three, GROUPS))
    mixed_empty = jnp.take_along_axis(surplus_rows, random_permute, axis=1)
    far_surplus = jnp.where(device_ids[None, :] < half_devices, surplus_rows, 0)
    far_empty = jnp.roll(far_surplus, half_devices, axis=1)
    chosen_group = jax.random.randint(key_six, (), 0, GROUPS)
    use_far = (jax.random.randint(key_five, (GROUPS,), 0, 2) == 1) | (jnp.arange(GROUPS) == chosen_group)
    spare_count = jnp.where(use_far[:, None], far_surplus, surplus_rows)
    empty_slots = jnp.where(use_far[:, None], far_empty, mixed_empty)
    rank_order = jax.vmap(lambda subkey: jax.random.permutation(subkey, BLK_DEV))(jax.random.split(key_four, GROUPS * devices))
    rank_order = rank_order.reshape(GROUPS, devices, BLK_DEV)
    doubled = rank_order < spare_count[:, :, None]
    discarded_rows = (rank_order >= spare_count[:, :, None]) & (rank_order < (spare_count + empty_slots)[:, :, None])
    counts = 1 + doubled.astype(jnp.int32) - discarded_rows.astype(jnp.int32)
    return counts.reshape(GROUPS, NBLK).astype(jnp.int32)


def pair_masks(key, pairs):
    devices = NBLK // BLK_DEV
    key_one, key_two, key_three = jax.random.split(key, 3)
    number = jax.random.randint(key_one, (pairs, devices), 0, SWAPS + 1)
    forced = jax.random.randint(key_two, (pairs,), 0, devices)
    number = jnp.where(jnp.arange(devices)[None, :] == forced[:, None], SWAPS, number)
    rank_order = jax.vmap(lambda subkey: jax.random.permutation(subkey, BLK_DEV))(jax.random.split(key_three, pairs * devices))
    rank_order = rank_order.reshape(pairs, devices, BLK_DEV)
    return (rank_order < number[:, :, None]).astype(jnp.int32).reshape(pairs, NBLK)


def draw_even_pairs(key, part):
    return jnp.repeat(pair_masks(jax.random.fold_in(key, 11), GROUPS // 2), 2, axis=0)


def draw_odd_pairs(key, part):
    inner = jnp.repeat(pair_masks(jax.random.fold_in(key, 23), GROUPS // 2 - 1), 2, axis=0)
    border = jnp.zeros((1, NBLK), jnp.int32)
    return jnp.concatenate([border, inner, border], axis=0)


def shard_levels(stream_key, shape, shards, least, high):
    factor_of, own = 1.0, jax.random.fold_in(stream_key, 6)
    for dim, shards_of in shards:
        steps = jnp.exp(jax.random.uniform(jax.random.fold_in(own, dim), (shards_of,), jnp.float32, least / len(shards), high / len(shards)))
        factor_of = factor_of * jnp.repeat(steps, shape[dim] // shards_of).reshape([-1 if axis == dim else 1 for axis in range(len(shape))])
    return factor_of


def centred(rng, dims, scale, limit, pieces=(), kind=jnp.bfloat16):
    drawn = scale * jax.random.normal(rng, dims, jnp.float32)
    if pieces:
        drawn = drawn * shard_levels(rng, dims, pieces, -0.22, 0.18)
    return jnp.clip(drawn, -limit, limit).astype(kind)


def setup_inputs(seed: int = 0) -> dict:
    key_of = jax.random.split(jax.random.key(seed), 13)
    particles = centred(key_of[0], (GROUPS, PARTICLES, DIM), 1.0, 6.0, ((0, 4), (1, 8)))
    log_weights = draw_log_weights(jax.random.fold_in(key_of[12], 71), 0)
    offspring = draw_offspring(jax.random.fold_in(key_of[12], 71), 0)
    even_pairs = draw_even_pairs(jax.random.fold_in(key_of[12], 71), 0)
    odd_pairs = draw_odd_pairs(jax.random.fold_in(key_of[12], 71), 0)
    inverse_temp = jnp.clip(jnp.exp(math.log(4.0) - 2.0794415 * jax.random.uniform(key_of[5], (GROUPS,), jnp.float32) ** shard_levels(key_of[5], (GROUPS,), ((0, 4),), -0.2, 0.2)), 0.5, 4.0)
    flow_in = centred(key_of[6], (DIM // 2, HID), (DIM // 2) ** -0.5, 0.15625)
    flow_mid = centred(key_of[7], (HID, HID), HID ** -0.5, 0.25)
    flow_out = centred(key_of[8], (HID, DIM), HID ** -0.5, 0.25)
    energy_in = centred(key_of[9], (DIM, HID), DIM ** -0.5, 0.109375)
    energy_mid = centred(key_of[10], (HID, HID), HID ** -0.5, 0.25)
    energy_out = centred(key_of[11], (HID,), HID ** -0.5, 0.25, (), jnp.float32)
    return dict(particles=particles, log_weights=log_weights, offspring=offspring, even_pairs=even_pairs, odd_pairs=odd_pairs, inverse_temp=inverse_temp, flow_in=flow_in, flow_mid=flow_mid, flow_out=flow_out, energy_in=energy_in, energy_mid=energy_mid, energy_out=energy_out)


old_level = 0.5
new_level = 0.75
scale_limit = 0.05


def transport(row_data, flow_in, flow_mid, flow_out):
    half_width = row_data.shape[1] // 2
    kept_half = row_data[:, :half_width]
    moved_half = row_data[:, half_width:]
    hidden_one = jax.nn.gelu(jnp.dot(kept_half, flow_in, preferred_element_type=jnp.float32)).astype(jnp.bfloat16)
    hidden_two = jax.nn.gelu(jnp.dot(hidden_one, flow_mid, preferred_element_type=jnp.float32)).astype(jnp.bfloat16)
    scale_shift = jnp.dot(hidden_two, flow_out, preferred_element_type=jnp.float32)
    log_scale = scale_limit * jnp.tanh(scale_shift[:, :half_width])
    offset_rows = (moved_half.astype(jnp.float32) * jnp.exp(log_scale) + scale_shift[:, half_width:]).astype(jnp.bfloat16)
    return jnp.concatenate([kept_half, offset_rows], axis=1), jnp.sum(log_scale, axis=1)


def energy(row_data, energy_in, energy_mid, energy_out):
    layer_one = jax.nn.gelu(jnp.dot(row_data, energy_in, preferred_element_type=jnp.float32)).astype(jnp.bfloat16)
    layer_two = jax.nn.gelu(jnp.dot(layer_one, energy_mid, preferred_element_type=jnp.float32))
    return jnp.sum(layer_two * energy_out[None, :], axis=1)


def resample_group(blocks, weights, counts):
    doubled = (counts == 2).astype(jnp.int32)
    discarded_rows = (counts == 0).astype(jnp.int32)
    spare_rank = jnp.cumsum(doubled) - 1
    vacant_rank = jnp.cumsum(discarded_rows) - 1
    positions = jnp.arange(counts.shape[0], dtype=jnp.int32)
    matches = (doubled[None, :] == 1) & (spare_rank[None, :] == vacant_rank[:, None])
    source = jnp.sum(jnp.where(matches, positions[None, :], 0), axis=1).astype(jnp.int32)
    weights = weights - jnp.log(jnp.maximum(counts, 1).astype(jnp.float32))[:, None]
    vacant = discarded_rows == 1
    blocks = jnp.where(vacant[:, None, None], jnp.take(blocks, source, axis=0), blocks)
    weights = jnp.where(vacant[:, None], jnp.take(weights, source, axis=0), weights)
    return blocks, weights


def reference(particles, log_weights, offspring, even_pairs, odd_pairs, inverse_temp, flow_in, flow_mid, flow_out, energy_in, energy_mid, energy_out):
    groups = particles.shape[0]
    block_count = offspring.shape[1]
    block_rows = particles.shape[1] // block_count
    features = particles.shape[2]
    blocks = particles.reshape(groups, block_count, block_rows, features)
    weights = log_weights.reshape(groups, block_count, block_rows)
    blocks, weights = jax.vmap(resample_group)(blocks, weights, offspring)
    group_ids = jnp.arange(groups, dtype=jnp.int32)
    even_partner = group_ids + 1 - 2 * (group_ids % 2)
    odd_partner = jnp.clip(group_ids - 1 + 2 * (group_ids % 2), 0, groups - 1)
    blocks = jnp.where((even_pairs == 1)[:, :, None, None], jnp.take(blocks, even_partner, axis=0), blocks)
    blocks = jnp.where((odd_pairs == 1)[:, :, None, None], jnp.take(blocks, odd_partner, axis=0), blocks)
    row_data = blocks.reshape(groups, block_count * block_rows, features)

    def per_group(item):
        rows_in = item
        moved, log_det = transport(rows_in, flow_in, flow_mid, flow_out)
        before = energy(rows_in, energy_in, energy_mid, energy_out)
        after = energy(moved, energy_in, energy_mid, energy_out)
        return moved, log_det, before, after

    moved, log_det, before, after = lax.map(per_group, row_data)
    updated = weights.reshape(groups, -1) + log_det - inverse_temp[:, None] * (new_level * after - old_level * before)
    peak = jnp.max(updated, axis=1)
    first_sum = jnp.sum(jnp.exp(updated - peak[:, None]), axis=1)
    second_sum = jnp.sum(jnp.exp(2.0 * (updated - peak[:, None])), axis=1)
    new_log_weights = updated - (peak + jnp.log(first_sum))[:, None]
    log_ess = 2.0 * jnp.log(first_sum) - jnp.log(second_sum) - jnp.log(jnp.float32(updated.shape[1]))
    return moved, new_log_weights, log_ess
```

```python
import functools

import jax
import jax.numpy as jnp
from jax import lax
from jax.experimental import pallas as pl
from jax.experimental.pallas import tpu as pltpu
from jax.sharding import PartitionSpec as P

SWAPS = 2
LANES = 128
TILE = 256

old_level = 0.5
new_level = 0.75
scale_limit = 0.05
MESH = pl.DeviceIdType.MESH


def gelu(x):
    return 0.5 * x * (1.0 + jnp.tanh(0.7978845608028654 * (x + 0.044715 * (x * x * x))))


def dot(a, b):
    return jnp.dot(a, b, preferred_element_type=jnp.float32)


def fold(x):
    total = x[:, :LANES]
    for c in range(LANES, x.shape[1], LANES):
        total = total + x[:, c : c + LANES]
    return total


def lane_sums(x):
    return [
        jnp.sum(jnp.transpose(x[i : i + LANES]), axis=0, keepdims=True)
        for i in range(0, x.shape[0], LANES)
    ]


def kernel(
    n,
    groups,
    nb,
    off,
    even,
    odd,
    inv,
    logw,
    eout,
    part,
    fin,
    fmid,
    fout,
    ein,
    emid,
    out,
    nlw,
    ess,
    p0,
    p1,
    n1,
    wfin,
    wfmid,
    wfout,
    wein,
    wemid,
    g0,
    g1,
    es0,
    es1,
    er0,
    er1,
    os0,
    os1,
    or0,
    or1,
    tal,
    tals,
    tg,
    qg,
    xes,
    xer,
    xos,
    xor_,
    load_sem,
    smem_sem,
    ring_send,
    ring_recv,
    all_send,
    all_recv,
    swap_send,
    swap_recv,
    tiny_send,
    tiny_recv,
):
    br = part.shape[1]
    half = part.shape[2] // 2
    rows = nb * br
    per = LANES // br
    srows = rows // LANES
    me = lax.axis_index("dom")
    grp = lax.axis_index("temp")
    has_odd = (grp > 0) & (grp < groups - 1)
    even_dev = grp + 1 - 2 * (grp % 2)
    odd_dev = grp - 1 + 2 * (grp % 2)

    loads = [
        pltpu.make_async_copy(part.at[:, :, pl.ds(0, half)], p0.at[pl.ds(0, nb)], load_sem.at[0]),
        pltpu.make_async_copy(fin, wfin, load_sem.at[1]),
        pltpu.make_async_copy(fmid, wfmid, load_sem.at[2]),
        pltpu.make_async_copy(fout, wfout, load_sem.at[3]),
        pltpu.make_async_copy(part.at[:, :, pl.ds(half, half)], p1, load_sem.at[4]),
        pltpu.make_async_copy(ein, wein, load_sem.at[5]),
        pltpu.make_async_copy(emid, wemid, load_sem.at[6]),
    ]
    for c in loads:
        c.start()

    for ref in (or0, or1, xor_):
        ref[...] = jnp.zeros(ref.shape, ref.dtype)

    barrier = pltpu.get_barrier_semaphore()
    for k in range(1, n):
        pl.semaphore_signal(
            barrier, inc=1, device_id={"dom": lax.rem(me + k, n)}, device_id_type=MESH
        )
    pl.semaphore_signal(barrier, inc=1, device_id={"temp": even_dev}, device_id_type=MESH)

    @pl.when(has_odd)
    def _():
        pl.semaphore_signal(barrier, inc=1, device_id={"temp": odd_dev}, device_id_type=MESH)

    spare = jnp.int32(0)
    vacant = jnp.int32(-1)
    dd = jnp.int32(0)
    vv = jnp.int32(0)
    cnt = [off[0, j] for j in range(nb)]
    ev = [even[0, j] for j in range(nb)]
    od = [odd[0, j] for j in range(nb)]
    for j in range(nb):
        spare = jnp.where(cnt[j] == 2, j, spare)
        vacant = jnp.where(cnt[j] == 0, j, vacant)
        dd = jnp.where(cnt[j] == 2, 1, dd)
        vv = jnp.where(cnt[j] == 0, 1, vv)

    def ranks(flags):
        seen = jnp.int32(0)
        rank = []
        chosen = [jnp.int32(0)] * SWAPS
        for j in range(nb):
            rank.append(jnp.minimum(seen, SWAPS - 1))
            for s in range(SWAPS):
                chosen[s] = jnp.where((flags[j] == 1) & (seen == s), j, chosen[s])
            seen = seen + flags[j]
        return rank, chosen

    erank, echosen = ranks(ev)
    orank, ochosen = ranks(od)

    def pick(values, index):
        total = values[0]
        for j in range(1, len(values)):
            total = jnp.where(index == j, values[j], total)
        return total

    loads[0].wait()
    g0[me] = p0[spare]
    tal[me] = jnp.full((8, LANES), dd + 2 * vv, jnp.int32)

    @pl.when(has_odd)
    def _():
        pl.semaphore_wait(barrier, n + 1)

    @pl.when(jnp.logical_not(has_odd))
    def _():
        pl.semaphore_wait(barrier, n)

    odd_me = me % 2
    pos = (1 - odd_me) * (me // 2) + odd_me * (n - 1 - me // 2)

    def dom_of(p):
        p = (p + 2 * n) % n
        hi = p // (n // 2)
        return (1 - hi) * (2 * p) + hi * (2 * (n - 1 - p) + 1)

    g = (g0, g1)
    steps = n - 1
    cr = br // 2

    def ring_copy(h, way, s, receiving):
        d = s // 2 + 1
        r = (s % 2 + way) % 2
        sign = 1 - 2 * way
        owner = dom_of(pos - sign * (d if receiving else d - 1))
        view = g[h].at[owner, pl.ds(r * cr, cr)]
        return pltpu.make_async_remote_copy(
            src_ref=view,
            dst_ref=view,
            send_sem=ring_send.at[h, way, s],
            recv_sem=ring_recv.at[h, way, s],
            device_id={"dom": dom_of(pos + sign)},
            device_id_type=MESH,
        )

    def ring_step(h, s):
        for way in range(2):
            if s >= 2:
                ring_copy(h, way, s - 2, True).wait_recv()
            ring_copy(h, way, s, False).start()

    def ring_end(h):
        for s in range(max(steps - 2, 0), steps):
            for way in range(2):
                ring_copy(h, way, s, True).wait_recv()

    pending = [(0, s) for s in range(steps)]

    def pump(count):
        for _ in range(min(count, len(pending))):
            ring_step(*pending.pop(0))

    def share(index, ref, receiving, k):
        view = ref.at[lax.rem(me - k + n, n)] if receiving else ref.at[me]
        return pltpu.make_async_remote_copy(
            src_ref=view,
            dst_ref=view,
            send_sem=all_send.at[index, k],
            recv_sem=all_recv.at[index, k],
            device_id={"dom": lax.rem(me + k, n)},
            device_id_type=MESH,
        )

    def share_start(index, ref):
        for k in range(1, n):
            share(index, ref, False, k).start()

    def share_wait(index, ref):
        for k in range(1, n):
            share(index, ref, True, k).wait_recv()

    pump(2)
    share_start(0, tal)

    tiles = rows // TILE
    lds = []
    wide = 512
    for c in loads[1:5]:
        c.wait()
    tb = TILE // br

    def tall(ref, t, cols=slice(None)):
        x = ref[t * tb : (t + 1) * tb, :, cols]
        return x.reshape(TILE, x.shape[2])

    for t in range(tiles):
        rs = slice(t * tb, (t + 1) * tb)
        hid = gelu(dot(tall(p0, t), wfin[...])).astype(jnp.bfloat16)
        hid = gelu(dot(hid, wfmid[...])).astype(jnp.bfloat16)
        total = jnp.zeros((TILE, LANES), jnp.float32)
        for c in range(0, half, wide):
            ls = scale_limit * jnp.tanh(dot(hid, wfout[:, c : c + wide]))
            shift = dot(hid, wfout[:, half + c : half + c + wide])
            new = tall(p1, t, slice(c, c + wide)).astype(jnp.float32) * jnp.exp(ls) + shift
            n1[rs, :, c : c + wide] = new.astype(jnp.bfloat16).reshape(tb, br, wide)
            total = total + fold(ls)
        lds += lane_sums(total)
        pump(1)
    g1[me] = n1[spare]
    pending += [(1, s) for s in range(steps)]

    share_wait(0, tal)
    down = pltpu.make_async_copy(tal, tals, smem_sem)
    down.start()
    down.wait()
    my_rank = jnp.int32(0)
    codes = [tals[o, 0, 0] for o in range(n)]
    for o in range(n):
        my_rank = my_rank + jnp.where(o < me, codes[o] // 2, 0)
    source = jnp.int32(0)
    seen = jnp.int32(0)
    for o in range(n):
        has = codes[o] % 2
        source = jnp.where((has == 1) & (seen == my_rank), o, source)
        seen = seen + has

    loads[5].wait()
    loads[6].wait()
    us = []
    for t in range(tiles):
        low = dot(tall(p0, t), wein[:half, :])

        def energy(v, low):
            layer = gelu(low + dot(v, wein[half:, :])).astype(jnp.bfloat16)
            return fold(gelu(dot(layer, wemid[...])) * eout[...])

        before = energy(tall(p1, t), low)
        pump(1)
        after = energy(tall(n1, t), low)
        us += lane_sums(new_level * after - old_level * before)
        pump(1)

    lane = lax.broadcasted_iota(jnp.int32, (srows, LANES), 1)
    row = lax.broadcasted_iota(jnp.int32, (srows, LANES), 0)
    slot = row * per + lane // br

    def spread(values):
        total = jnp.zeros((srows, LANES), jnp.int32)
        for j in range(nb):
            total = jnp.where(slot == j, values[j], total)
        return total

    counts = spread(cnt)
    kept = logw[...] - jnp.log(jnp.maximum(counts, 1).astype(jnp.float32))
    mine = tg.at[me]
    tg[me] = jnp.zeros((tg.shape[1], LANES), jnp.float32)
    for i in range(srows):
        mine[i : i + 1, :] = lds[i]
        mine[srows + i : srows + i + 1, :] = us[i]
    own_ld = mine[0:srows, :]
    own_u = mine[srows : 2 * srows, :]
    lane1 = lax.broadcasted_iota(jnp.int32, (1, LANES), 1)
    for i, values in enumerate((own_ld, own_u, kept)):
        v = pick([values[j : j + 1, :] for j in range(srows)], spare // per)
        turned = pltpu.roll(v, br, 1)
        mine[2 * srows + i : 2 * srows + i + 1, :] = jnp.where(
            lane1 // br == spare % per, v, turned
        )
    share_start(1, tg)
    pump(1)
    share_wait(1, tg)
    fill = tg[source]
    vmask = slot == vacant

    def filled(i, values):
        return jnp.where(
            vmask, jnp.broadcast_to(fill[2 * srows + i : 2 * srows + i + 1, :], values.shape), values
        )

    ld = filled(0, own_ld)
    u = filled(1, own_u)
    weight = filled(2, kept)

    def swap_copy(index, sems, src, dst, device):
        return pltpu.make_async_remote_copy(
            src_ref=src,
            dst_ref=dst,
            send_sem=sems[0].at[index],
            recv_sem=sems[1].at[index],
            device_id={"temp": device},
            device_id_type=MESH,
        )

    tiny = (tiny_send, tiny_recv)
    big = (swap_send, swap_recv)
    xes[0:srows, :] = ld
    xes[srows : 2 * srows, :] = u
    tiny_even = swap_copy(0, tiny, xes, xer, even_dev)
    tiny_even.start()
    emask = spread(ev) == 1
    omask = spread(od) == 1
    pump(1)
    tiny_even.wait()
    ld = jnp.where(emask, xer[0:srows, :], ld)
    u = jnp.where(emask, xer[srows : 2 * srows, :], u)
    xos[0:srows, :] = ld
    xos[srows : 2 * srows, :] = u
    tiny_odd = swap_copy(1, tiny, xos, xor_, odd_dev)

    stock = (p0, n1)
    sends_e, gets_e = (es0, es1), (er0, er1)
    sends_o, gets_o = (os0, os1), (or0, or1)
    resampled = [jnp.where(cnt[j] == 0, nb, j) for j in range(nb)]
    evened = [jnp.where(ev[j] == 1, nb + 1 + erank[j], resampled[j]) for j in range(nb)]
    final = [jnp.where(od[j] == 1, nb + 1 + SWAPS + orank[j], evened[j]) for j in range(nb)]

    def even_copy(h):
        return swap_copy(h, big, sends_e[h], gets_e[h], even_dev)

    def odd_copy(h):
        return swap_copy(2 + h, big, sends_o[h], gets_o[h], odd_dev)

    def even_send(h):
        stock[h][nb] = g[h][source]
        for s in range(SWAPS):
            sends_e[h][s] = stock[h][pick(resampled, echosen[s])]
        even_copy(h).start()

    def odd_send(h):
        even_copy(h).wait()
        stock[h][nb + 1 : nb + 1 + SWAPS] = gets_e[h][...]
        for s in range(SWAPS):
            sends_o[h][s] = stock[h][pick(evened, ochosen[s])]

        @pl.when(has_odd)
        def _():
            odd_copy(h).start()

    def finish(h):
        @pl.when(has_odd)
        def _():
            odd_copy(h).wait()

        stock[h][nb + 1 + SWAPS :] = gets_o[h][...]
        for j in range(nb):
            out[j, :, h * half : (h + 1) * half] = stock[h][final[j]]

    ring_end(0)
    even_send(0)

    @pl.when(has_odd)
    def _():
        tiny_odd.start()

    pump(1)
    odd_send(0)
    pump(1)

    @pl.when(has_odd)
    def _():
        tiny_odd.wait()

    ld = jnp.where(omask, xor_[0:srows, :], ld)
    u = jnp.where(omask, xor_[srows : 2 * srows, :], u)
    updated = weight + ld - inv[0] * u

    def everywhere(x):
        return jnp.broadcast_to(x, (1, LANES))

    def whole(reduce, x):
        return everywhere(reduce(reduce(x, axis=0, keepdims=True), axis=1, keepdims=True))

    own_peak = whole(jnp.max, updated)
    qmine = qg.at[me]
    qg[me] = jnp.zeros((qg.shape[1], LANES), jnp.float32)
    qmine[0:1, :] = own_peak
    qmine[1:2, :] = whole(jnp.sum, jnp.exp(updated - own_peak))
    qmine[2:3, :] = whole(jnp.sum, jnp.exp(2.0 * (updated - own_peak)))
    share_start(2, qg)
    pump(1)
    finish(0)
    pump(1)
    share_wait(2, qg)
    pump(len(pending))
    peak = qg[0, 0:1, :]
    for o in range(1, n):
        peak = jnp.maximum(peak, qg[o, 0:1, :])
    first = jnp.zeros((1, LANES), jnp.float32)
    second = jnp.zeros((1, LANES), jnp.float32)
    for o in range(n):
        lower = qg[o, 0:1, :] - peak
        first = first + qg[o, 1:2, :] * jnp.exp(lower)
        second = second + qg[o, 2:3, :] * jnp.exp(2.0 * lower)
    nlw[...] = updated - (peak + jnp.log(first))
    total = jnp.full((1, LANES), float(rows * n), jnp.float32)
    ess[...] = 2.0 * jnp.log(first) - jnp.log(second) - jnp.log(total)

    ring_end(1)
    even_send(1)
    odd_send(1)
    finish(1)

    for h in range(2):
        for s in range(steps):
            for way in range(2):
                ring_copy(h, way, s, False).wait_send()
    for index, ref in enumerate((tal, tg, qg)):
        for k in range(1, n):
            share(index, ref, False, k).wait_send()


def per_device(
    particles,
    log_weights,
    offspring,
    even_pairs,
    odd_pairs,
    inverse_temp,
    flow_in,
    flow_mid,
    flow_out,
    energy_in,
    energy_mid,
    energy_out,
):
    n = lax.axis_size("dom")
    groups = lax.axis_size("temp")
    nb = offspring.shape[1]
    rows, features = particles.shape[1:]
    half = features // 2
    br = rows // nb
    srows = rows // LANES
    hid = flow_mid.shape[0]
    bf16, f32, i32 = jnp.bfloat16, jnp.float32, jnp.int32
    smem = pl.BlockSpec(memory_space=pltpu.SMEM)
    vmem = pl.BlockSpec(memory_space=pltpu.VMEM)
    anywhere = pl.BlockSpec(memory_space=pl.ANY)
    tile_rows = -(-(2 * srows + 3) // 8) * 8
    pair_rows = -(-(2 * srows) // 8) * 8
    swap = pltpu.VMEM((SWAPS, br, half), bf16)
    dma = pltpu.SemaphoreType.DMA
    moved, weights, ess = pl.pallas_call(
        functools.partial(kernel, n, groups, nb),
        out_shape=(
            jax.ShapeDtypeStruct((nb, br, features), bf16),
            jax.ShapeDtypeStruct((srows, LANES), f32),
            jax.ShapeDtypeStruct((1, LANES), f32),
        ),
        in_specs=[smem] * 4 + [vmem] * 2 + [anywhere] * 6,
        out_specs=(vmem, vmem, vmem),
        scratch_shapes=[
            pltpu.VMEM((nb + 1 + 2 * SWAPS, br, half), bf16),
            pltpu.VMEM((nb, br, half), bf16),
            pltpu.VMEM((nb + 1 + 2 * SWAPS, br, half), bf16),
            pltpu.VMEM(flow_in.shape, bf16),
            pltpu.VMEM(flow_mid.shape, bf16),
            pltpu.VMEM(flow_out.shape, bf16),
            pltpu.VMEM(energy_in.shape, bf16),
            pltpu.VMEM(energy_mid.shape, bf16),
            pltpu.VMEM((n, br, half), bf16),
            pltpu.VMEM((n, br, half), bf16),
        ]
        + [swap] * 8
        + [
            pltpu.VMEM((n, 8, LANES), i32),
            pltpu.SMEM((n, 8, LANES), i32),
            pltpu.VMEM((n, tile_rows, LANES), f32),
            pltpu.VMEM((n, 8, LANES), f32),
        ]
        + [pltpu.VMEM((pair_rows, LANES), f32)] * 4
        + [
            dma((7,)),
            dma,
            dma((2, 2, n - 1)),
            dma((2, 2, n - 1)),
            dma((3, n)),
            dma((3, n)),
            dma((4,)),
            dma((4,)),
            dma((2,)),
            dma((2,)),
        ],
        compiler_params=pltpu.CompilerParams(
            collective_id=0, has_side_effects=True, vmem_limit_bytes=56 * 1024 * 1024
        ),
    )(
        offspring,
        even_pairs,
        odd_pairs,
        inverse_temp,
        log_weights.reshape(srows, LANES),
        energy_out.reshape(1, hid),
        particles.reshape(nb, br, features),
        flow_in,
        flow_mid,
        flow_out,
        energy_in,
        energy_mid,
    )
    return (
        moved.reshape(1, rows, features),
        weights.reshape(1, rows),
        ess[0, :1],
    )


def solution(mesh):
    in_specs = (
        P("temp", "dom", None),
        P("temp", "dom"),
        P("temp", "dom"),
        P("temp", "dom"),
        P("temp", "dom"),
        P("temp"),
        P(),
        P(),
        P(),
        P(),
        P(),
        P(),
    )
    out_specs = (P("temp", "dom", None), P("temp", "dom"), P("temp"))
    return jax.shard_map(
        per_device, mesh=mesh, in_specs=in_specs, out_specs=out_specs, check_vma=False
    )
```

```python
import functools

import jax
import jax.numpy as jnp
from jax import lax
from jax.experimental import pallas as pl
from jax.experimental.pallas import tpu as pltpu
from jax.sharding import PartitionSpec as P

SWAPS = 2
LANES = 128
TILE = 256

old_level = 0.5
new_level = 0.75
scale_limit = 0.05
MESH = pl.DeviceIdType.MESH


def gelu(x):
    return 0.5 * x * (1.0 + jnp.tanh(0.7978845608028654 * (x + 0.044715 * (x * x * x))))


def dot(a, b):
    return jnp.dot(a, b, preferred_element_type=jnp.float32)


def fold(x):
    total = x[:, :LANES]
    for c in range(LANES, x.shape[1], LANES):
        total = total + x[:, c : c + LANES]
    return total


def lane_sums(x):
    return [
        jnp.sum(jnp.transpose(x[i : i + LANES]), axis=0, keepdims=True)
        for i in range(0, x.shape[0], LANES)
    ]


def kernel(
    n,
    groups,
    nb,
    off,
    even,
    odd,
    inv,
    logw,
    eout,
    part,
    fin,
    fmid,
    fout,
    ein,
    emid,
    out,
    nlw,
    ess,
    p0,
    p1,
    n1,
    wfin,
    wfmid,
    wfout,
    wein,
    wemid,
    g0,
    g1,
    es0,
    es1,
    er0,
    er1,
    os0,
    os1,
    or0,
    or1,
    tal,
    tals,
    tg,
    qg,
    xes,
    xer,
    xos,
    xor_,
    load_sem,
    smem_sem,
    ring_send,
    ring_recv,
    all_send,
    all_recv,
    swap_send,
    swap_recv,
    tiny_send,
    tiny_recv,
):
    br = part.shape[1]
    half = part.shape[2] // 2
    rows = nb * br
    per = LANES // br
    srows = rows // LANES
    me = lax.axis_index("dom")
    grp = lax.axis_index("temp")
    has_odd = (grp > 0) & (grp < groups - 1)
    even_dev = grp + 1 - 2 * (grp % 2)
    odd_dev = grp - 1 + 2 * (grp % 2)

    loads = [
        pltpu.make_async_copy(part.at[:, :, pl.ds(0, half)], p0.at[pl.ds(0, nb)], load_sem.at[0]),
        pltpu.make_async_copy(fin, wfin, load_sem.at[1]),
        pltpu.make_async_copy(fmid, wfmid, load_sem.at[2]),
        pltpu.make_async_copy(fout, wfout, load_sem.at[3]),
        pltpu.make_async_copy(part.at[:, :, pl.ds(half, half)], p1, load_sem.at[4]),
        pltpu.make_async_copy(ein, wein, load_sem.at[5]),
        pltpu.make_async_copy(emid, wemid, load_sem.at[6]),
    ]
    for c in loads:
        c.start()

    for ref in (or0, or1, xor_):
        ref[...] = jnp.zeros(ref.shape, ref.dtype)

    barrier = pltpu.get_barrier_semaphore()
    for k in range(1, n):
        pl.semaphore_signal(
            barrier, inc=1, device_id={"dom": lax.rem(me + k, n)}, device_id_type=MESH
        )
    pl.semaphore_signal(barrier, inc=1, device_id={"temp": even_dev}, device_id_type=MESH)

    @pl.when(has_odd)
    def _():
        pl.semaphore_signal(barrier, inc=1, device_id={"temp": odd_dev}, device_id_type=MESH)

    spare = jnp.int32(0)
    vacant = jnp.int32(-1)
    dd = jnp.int32(0)
    vv = jnp.int32(0)
    cnt = [off[0, j] for j in range(nb)]
    ev = [even[0, j] for j in range(nb)]
    od = [odd[0, j] for j in range(nb)]
    for j in range(nb):
        spare = jnp.where(cnt[j] == 2, j, spare)
        vacant = jnp.where(cnt[j] == 0, j, vacant)
        dd = jnp.where(cnt[j] == 2, 1, dd)
        vv = jnp.where(cnt[j] == 0, 1, vv)

    def ranks(flags):
        seen = jnp.int32(0)
        rank = []
        chosen = [jnp.int32(0)] * SWAPS
        for j in range(nb):
            rank.append(jnp.minimum(seen, SWAPS - 1))
            for s in range(SWAPS):
                chosen[s] = jnp.where((flags[j] == 1) & (seen == s), j, chosen[s])
            seen = seen + flags[j]
        return rank, chosen

    erank, echosen = ranks(ev)
    orank, ochosen = ranks(od)

    def pick(values, index):
        total = values[0]
        for j in range(1, len(values)):
            total = jnp.where(index == j, values[j], total)
        return total

    loads[0].wait()
    g0[me] = p0[spare]
    tal[me] = jnp.full((8, LANES), dd + 2 * vv, jnp.int32)

    @pl.when(has_odd)
    def _():
        pl.semaphore_wait(barrier, n + 1)

    @pl.when(jnp.logical_not(has_odd))
    def _():
        pl.semaphore_wait(barrier, n)

    odd_me = me % 2
    pos = (1 - odd_me) * (me // 2) + odd_me * (n - 1 - me // 2)

    def dom_of(p):
        p = (p + 2 * n) % n
        hi = p // (n // 2)
        return (1 - hi) * (2 * p) + hi * (2 * (n - 1 - p) + 1)

    g = (g0, g1)
    steps = n - 1
    cr = br // 2

    def ring_copy(h, way, s, receiving):
        d = s // 2 + 1
        r = (s % 2 + way) % 2
        sign = 1 - 2 * way
        owner = dom_of(pos - sign * (d if receiving else d - 1))
        view = g[h].at[owner, pl.ds(r * cr, cr)]
        return pltpu.make_async_remote_copy(
            src_ref=view,
            dst_ref=view,
            send_sem=ring_send.at[h, way, s],
            recv_sem=ring_recv.at[h, way, s],
            device_id={"dom": dom_of(pos + sign)},
            device_id_type=MESH,
        )

    def ring_step(h, s):
        for way in range(2):
            if s >= 2:
                ring_copy(h, way, s - 2, True).wait_recv()
            ring_copy(h, way, s, False).start()

    def ring_end(h):
        for s in range(max(steps - 2, 0), steps):
            for way in range(2):
                ring_copy(h, way, s, True).wait_recv()

    pending = [(0, s) for s in range(steps)]

    def pump(count):
        for _ in range(min(count, len(pending))):
            ring_step(*pending.pop(0))

    def share(index, ref, receiving, k):
        view = ref.at[lax.rem(me - k + n, n)] if receiving else ref.at[me]
        return pltpu.make_async_remote_copy(
            src_ref=view,
            dst_ref=view,
            send_sem=all_send.at[index, k],
            recv_sem=all_recv.at[index, k],
            device_id={"dom": lax.rem(me + k, n)},
            device_id_type=MESH,
        )

    def share_start(index, ref):
        for k in range(1, n):
            share(index, ref, False, k).start()

    def share_wait(index, ref):
        for k in range(1, n):
            share(index, ref, True, k).wait_recv()

    pump(2)
    share_start(0, tal)

    tiles = rows // TILE
    lds = []
    wide = 512
    for c in loads[1:5]:
        c.wait()
    tb = TILE // br

    def tall(ref, t, cols=slice(None)):
        x = ref[t * tb : (t + 1) * tb, :, cols]
        return x.reshape(TILE, x.shape[2])

    for t in range(tiles):
        rs = slice(t * tb, (t + 1) * tb)
        hid = gelu(dot(tall(p0, t), wfin[...])).astype(jnp.bfloat16)
        hid = gelu(dot(hid, wfmid[...])).astype(jnp.bfloat16)
        pump(1)
        total = jnp.zeros((TILE, LANES), jnp.float32)
        for c in range(0, half, wide):
            ls = scale_limit * jnp.tanh(dot(hid, wfout[:, c : c + wide]))
            shift = dot(hid, wfout[:, half + c : half + c + wide])
            new = tall(p1, t, slice(c, c + wide)).astype(jnp.float32) * jnp.exp(ls) + shift
            n1[rs, :, c : c + wide] = new.astype(jnp.bfloat16).reshape(tb, br, wide)
            total = total + fold(ls)
        lds += lane_sums(total)
        pump(1)
    g1[me] = n1[spare]
    pending += [(1, s) for s in range(steps)]

    share_wait(0, tal)
    down = pltpu.make_async_copy(tal, tals, smem_sem)
    down.start()
    down.wait()
    my_rank = jnp.int32(0)
    codes = [tals[o, 0, 0] for o in range(n)]
    for o in range(n):
        my_rank = my_rank + jnp.where(o < me, codes[o] // 2, 0)
    source = jnp.int32(0)
    seen = jnp.int32(0)
    for o in range(n):
        has = codes[o] % 2
        source = jnp.where((has == 1) & (seen == my_rank), o, source)
        seen = seen + has

    loads[5].wait()
    loads[6].wait()
    us = []
    for t in range(tiles):
        low = dot(tall(p0, t), wein[:half, :])

        def energy(v, low):
            layer = gelu(low + dot(v, wein[half:, :])).astype(jnp.bfloat16)
            return fold(gelu(dot(layer, wemid[...])) * eout[...])

        before = energy(tall(p1, t), low)
        pump(1)
        after = energy(tall(n1, t), low)
        us += lane_sums(new_level * after - old_level * before)
        pump(1)

    lane = lax.broadcasted_iota(jnp.int32, (srows, LANES), 1)
    row = lax.broadcasted_iota(jnp.int32, (srows, LANES), 0)
    slot = row * per + lane // br

    def spread(values):
        total = jnp.zeros((srows, LANES), jnp.int32)
        for j in range(nb):
            total = jnp.where(slot == j, values[j], total)
        return total

    counts = spread(cnt)
    kept = logw[...] - jnp.log(jnp.maximum(counts, 1).astype(jnp.float32))
    mine = tg.at[me]
    tg[me] = jnp.zeros((tg.shape[1], LANES), jnp.float32)
    for i in range(srows):
        mine[i : i + 1, :] = lds[i]
        mine[srows + i : srows + i + 1, :] = us[i]
    own_ld = mine[0:srows, :]
    own_u = mine[srows : 2 * srows, :]
    lane1 = lax.broadcasted_iota(jnp.int32, (1, LANES), 1)
    for i, values in enumerate((own_ld, own_u, kept)):
        v = pick([values[j : j + 1, :] for j in range(srows)], spare // per)
        turned = pltpu.roll(v, br, 1)
        mine[2 * srows + i : 2 * srows + i + 1, :] = jnp.where(
            lane1 // br == spare % per, v, turned
        )
    share_start(1, tg)
    pump(1)
    share_wait(1, tg)
    fill = tg[source]
    vmask = slot == vacant

    def filled(i, values):
        return jnp.where(
            vmask, jnp.broadcast_to(fill[2 * srows + i : 2 * srows + i + 1, :], values.shape), values
        )

    ld = filled(0, own_ld)
    u = filled(1, own_u)
    weight = filled(2, kept)

    def swap_copy(index, sems, src, dst, device):
        return pltpu.make_async_remote_copy(
            src_ref=src,
            dst_ref=dst,
            send_sem=sems[0].at[index],
            recv_sem=sems[1].at[index],
            device_id={"temp": device},
            device_id_type=MESH,
        )

    tiny = (tiny_send, tiny_recv)
    big = (swap_send, swap_recv)
    xes[0:srows, :] = ld
    xes[srows : 2 * srows, :] = u
    tiny_even = swap_copy(0, tiny, xes, xer, even_dev)
    tiny_even.start()
    emask = spread(ev) == 1
    omask = spread(od) == 1
    pump(1)
    tiny_even.wait()
    ld = jnp.where(emask, xer[0:srows, :], ld)
    u = jnp.where(emask, xer[srows : 2 * srows, :], u)
    xos[0:srows, :] = ld
    xos[srows : 2 * srows, :] = u
    tiny_odd = swap_copy(1, tiny, xos, xor_, odd_dev)

    stock = (p0, n1)
    sends_e, gets_e = (es0, es1), (er0, er1)
    sends_o, gets_o = (os0, os1), (or0, or1)
    resampled = [jnp.where(cnt[j] == 0, nb, j) for j in range(nb)]
    evened = [jnp.where(ev[j] == 1, nb + 1 + erank[j], resampled[j]) for j in range(nb)]
    final = [jnp.where(od[j] == 1, nb + 1 + SWAPS + orank[j], evened[j]) for j in range(nb)]

    def even_copy(h):
        return swap_copy(h, big, sends_e[h], gets_e[h], even_dev)

    def odd_copy(h):
        return swap_copy(2 + h, big, sends_o[h], gets_o[h], odd_dev)

    def even_send(h):
        stock[h][nb] = g[h][source]
        for s in range(SWAPS):
            sends_e[h][s] = stock[h][pick(resampled, echosen[s])]
        even_copy(h).start()

    def odd_send(h):
        even_copy(h).wait()
        stock[h][nb + 1 : nb + 1 + SWAPS] = gets_e[h][...]
        for s in range(SWAPS):
            sends_o[h][s] = stock[h][pick(evened, ochosen[s])]

        @pl.when(has_odd)
        def _():
            odd_copy(h).start()

    def finish(h):
        @pl.when(has_odd)
        def _():
            odd_copy(h).wait()

        stock[h][nb + 1 + SWAPS :] = gets_o[h][...]
        for j in range(nb):
            out[j, :, h * half : (h + 1) * half] = stock[h][final[j]]

    ring_end(0)
    even_send(0)

    @pl.when(has_odd)
    def _():
        tiny_odd.start()

    pump(1)
    odd_send(0)
    pump(1)

    @pl.when(has_odd)
    def _():
        tiny_odd.wait()

    ld = jnp.where(omask, xor_[0:srows, :], ld)
    u = jnp.where(omask, xor_[srows : 2 * srows, :], u)
    updated = weight + ld - inv[0] * u

    def everywhere(x):
        return jnp.broadcast_to(x, (1, LANES))

    def whole(reduce, x):
        return everywhere(reduce(reduce(x, axis=0, keepdims=True), axis=1, keepdims=True))

    own_peak = whole(jnp.max, updated)
    qmine = qg.at[me]
    qg[me] = jnp.zeros((qg.shape[1], LANES), jnp.float32)
    qmine[0:1, :] = own_peak
    qmine[1:2, :] = whole(jnp.sum, jnp.exp(updated - own_peak))
    qmine[2:3, :] = whole(jnp.sum, jnp.exp(2.0 * (updated - own_peak)))
    share_start(2, qg)
    pump(1)
    finish(0)
    pump(1)
    share_wait(2, qg)
    pump(len(pending))
    peak = qg[0, 0:1, :]
    for o in range(1, n):
        peak = jnp.maximum(peak, qg[o, 0:1, :])
    first = jnp.zeros((1, LANES), jnp.float32)
    second = jnp.zeros((1, LANES), jnp.float32)
    for o in range(n):
        lower = qg[o, 0:1, :] - peak
        first = first + qg[o, 1:2, :] * jnp.exp(lower)
        second = second + qg[o, 2:3, :] * jnp.exp(2.0 * lower)
    nlw[...] = updated - (peak + jnp.log(first))
    total = jnp.full((1, LANES), float(rows * n), jnp.float32)
    ess[...] = 2.0 * jnp.log(first) - jnp.log(second) - jnp.log(total)

    ring_end(1)
    even_send(1)
    odd_send(1)
    finish(1)

    for h in range(2):
        for s in range(steps):
            for way in range(2):
                ring_copy(h, way, s, False).wait_send()
    for index, ref in enumerate((tal, tg, qg)):
        for k in range(1, n):
            share(index, ref, False, k).wait_send()


def per_device(
    particles,
    log_weights,
    offspring,
    even_pairs,
    odd_pairs,
    inverse_temp,
    flow_in,
    flow_mid,
    flow_out,
    energy_in,
    energy_mid,
    energy_out,
):
    n = lax.axis_size("dom")
    groups = lax.axis_size("temp")
    nb = offspring.shape[1]
    rows, features = particles.shape[1:]
    half = features // 2
    br = rows // nb
    srows = rows // LANES
    hid = flow_mid.shape[0]
    bf16, f32, i32 = jnp.bfloat16, jnp.float32, jnp.int32
    smem = pl.BlockSpec(memory_space=pltpu.SMEM)
    vmem = pl.BlockSpec(memory_space=pltpu.VMEM)
    anywhere = pl.BlockSpec(memory_space=pl.ANY)
    tile_rows = -(-(2 * srows + 3) // 8) * 8
    pair_rows = -(-(2 * srows) // 8) * 8
    swap = pltpu.VMEM((SWAPS, br, half), bf16)
    dma = pltpu.SemaphoreType.DMA
    moved, weights, ess = pl.pallas_call(
        functools.partial(kernel, n, groups, nb),
        out_shape=(
            jax.ShapeDtypeStruct((nb, br, features), bf16),
            jax.ShapeDtypeStruct((srows, LANES), f32),
            jax.ShapeDtypeStruct((1, LANES), f32),
        ),
        in_specs=[smem] * 4 + [vmem] * 2 + [anywhere] * 6,
        out_specs=(vmem, vmem, vmem),
        scratch_shapes=[
            pltpu.VMEM((nb + 1 + 2 * SWAPS, br, half), bf16),
            pltpu.VMEM((nb, br, half), bf16),
            pltpu.VMEM((nb + 1 + 2 * SWAPS, br, half), bf16),
            pltpu.VMEM(flow_in.shape, bf16),
            pltpu.VMEM(flow_mid.shape, bf16),
            pltpu.VMEM(flow_out.shape, bf16),
            pltpu.VMEM(energy_in.shape, bf16),
            pltpu.VMEM(energy_mid.shape, bf16),
            pltpu.VMEM((n, br, half), bf16),
            pltpu.VMEM((n, br, half), bf16),
        ]
        + [swap] * 8
        + [
            pltpu.VMEM((n, 8, LANES), i32),
            pltpu.SMEM((n, 8, LANES), i32),
            pltpu.VMEM((n, tile_rows, LANES), f32),
            pltpu.VMEM((n, 8, LANES), f32),
        ]
        + [pltpu.VMEM((pair_rows, LANES), f32)] * 4
        + [
            dma((7,)),
            dma,
            dma((2, 2, n - 1)),
            dma((2, 2, n - 1)),
            dma((3, n)),
            dma((3, n)),
            dma((4,)),
            dma((4,)),
            dma((2,)),
            dma((2,)),
        ],
        compiler_params=pltpu.CompilerParams(
            collective_id=0, has_side_effects=True, vmem_limit_bytes=56 * 1024 * 1024
        ),
    )(
        offspring,
        even_pairs,
        odd_pairs,
        inverse_temp,
        log_weights.reshape(srows, LANES),
        energy_out.reshape(1, hid),
        particles.reshape(nb, br, features),
        flow_in,
        flow_mid,
        flow_out,
        energy_in,
        energy_mid,
    )
    return (
        moved.reshape(1, rows, features),
        weights.reshape(1, rows),
        ess[0, :1],
    )


def solution(mesh):
    in_specs = (
        P("temp", "dom", None),
        P("temp", "dom"),
        P("temp", "dom"),
        P("temp", "dom"),
        P("temp", "dom"),
        P("temp"),
        P(),
        P(),
        P(),
        P(),
        P(),
        P(),
    )
    out_specs = (P("temp", "dom", None), P("temp", "dom"), P("temp"))
    return jax.shard_map(
        per_device, mesh=mesh, in_specs=in_specs, out_specs=out_specs, check_vma=False
    )
```
